256 devices in a mesh: dp: 16 (over x_lo, y, core), vocab: 16 (over z, x_hi).
Axes of the slice: x: 4 (x_hi: 2, x_lo: 2; x = x_hi * 2 + x_lo), y: 4, z: 8, core: 2. Of those that a mesh axis runs over, the one named last changes fastest.
Arguments:
- teacher_hidden: bfloat16 [768, 16384], P('dp', 'vocab'), may hold values from -400 to 400
- teacher_gain: bfloat16 [16384], replicated, may hold values from 0.5 to 1.5
- teacher_unembed: bfloat16 [16384, 65536], P('dp', 'vocab'), may hold values from -12 to 12
- student_hidden: bfloat16 [768, 4096], P('dp', 'vocab'), may hold values from -400 to 400
- student_gain: bfloat16 [4096], replicated, may hold values from 0.5 to 1.5
- student_unembed: bfloat16 [4096, 65536], P('dp', 'vocab'), may hold values from -12 to 12
- labels: int32 [768], P('dp'), may hold values from 0 to 65535
Outputs:
- per_token_loss: float32 [768], P('dp')
- hidden_grad: float32 [768, 4096], P('dp', 'vocab')
- weight_grad: bfloat16 [4096, 65536], P('dp', 'vocab')
The draws below stay inside these ranges and needn't reach their ends.
All inputs are finite; a program needn't handle non-finite values.
Results may differ from the reference program's by a relative error of at most 0.012.
Values may be sent and summed in bfloat16 or wider, within the bound.
No kernel may reach another device: no remote copies, remote signals or barrier semaphores. Data moves between devices by JAX's collectives and lax.ppermute only.
A program may use at most 128 MiB of HBM per device.

```python
import math
import jax
import jax.numpy as jnp
import numpy as np
from jax import lax

DT = 16384
DS = 4096
TOKENS = 768
VOCAB = 65536


def scaled_rows(base_draw, row_key, col_key, row_top, feature_count):
    row_scale = jnp.exp(jax.random.uniform(row_key, (TOKENS, 1), jnp.float32, 0.0, math.log(row_top)))
    col_scale = jnp.exp(jax.random.uniform(col_key, (1, feature_count), jnp.float32, 0.0, math.log(10.0)))
    return base_draw * row_scale * col_scale


def scaled_columns(base_draw, col_key, rising, feature_count):
    col_scale = jnp.exp(jax.random.uniform(col_key, (1, VOCAB), jnp.float32, math.log(0.3), math.log(3.0)))
    return base_draw * feature_count ** (-0.5) * col_scale * rising[None, :]


def draw_teacher_hidden(key, part):
    key = jax.random.fold_in(key, 1)
    base_key, row_key, col_key = jax.random.split(key, 3)
    base_draw = jnp.clip(jax.random.normal(base_key, (TOKENS, DT), jnp.float32), -4.0, 4.0)
    row_top = 10.0
    drawn = scaled_rows(base_draw, row_key, col_key, row_top, DT)
    return drawn.astype(jnp.bfloat16)


def draw_student_hidden(key, part):
    key = jax.random.fold_in(key, 2)
    base_key, row_key, col_key = jax.random.split(key, 3)
    base_draw = jnp.clip(jax.random.normal(base_key, (TOKENS, DS), jnp.float32), -4.0, 4.0)
    row_top = 10.0
    drawn = scaled_rows(base_draw, row_key, col_key, row_top, DS)
    return drawn.astype(jnp.bfloat16)


def draw_teacher_unembed(key, part):
    key = jax.random.fold_in(key, 3)
    base_key, col_key = jax.random.split(key)
    position = jnp.arange(VOCAB, dtype=jnp.float32) / VOCAB
    base_draw = jnp.clip(jax.random.normal(base_key, (DT, VOCAB), jnp.float32), -3.0, 3.0)
    rising = 1.0 + 2.0 * position
    drawn = scaled_columns(base_draw, col_key, rising, DT)
    return drawn.astype(jnp.bfloat16)


def draw_student_unembed(key, part):
    key = jax.random.fold_in(key, 4)
    base_key, col_key = jax.random.split(key)
    position = jnp.arange(VOCAB, dtype=jnp.float32) / VOCAB
    base_draw = jnp.clip(jax.random.normal(base_key, (DS, VOCAB), jnp.float32), -3.0, 3.0)
    rising = 1.0 + 2.0 * position
    drawn = scaled_columns(base_draw, col_key, rising, DS)
    return drawn.astype(jnp.bfloat16)


def touch_ends(entries, stream_key, low, high):
    dims = entries.shape
    spot = [jax.random.randint(jax.random.fold_in(stream_key, axis), (), 0, dims[axis]) for axis in range(len(dims))]
    entries = entries.at[tuple(spot)].set(low)
    longest = dims.index(max(dims))
    spot[longest] = (spot[longest] + 1) % dims[longest]
    return entries.at[tuple(spot)].set(high)


def rank_table(number_of, lean):
    weights = [(1 << 20) // math.isqrt(rank ** lean) + 1 for rank in range(1, number_of + 1)]
    scale = 1 + sum(weights) // (1 << 30)
    return np.cumsum(np.array([max(1, weight // scale) for weight in weights]))


def ranked_ids(own_key, shape, count, slope):
    table = rank_table(count, slope)
    lot = jax.random.randint(jax.random.fold_in(own_key, 1), shape, 0, int(table[count - 1]))
    rank = jnp.searchsorted(jnp.asarray(table, jnp.int32), lot, side="right")
    return jax.random.permutation(jax.random.fold_in(own_key, 2), count)[rank].astype(jnp.int32)


def setup_inputs(seed: int = 0) -> dict:
    key_of = jax.random.split(jax.random.key(seed), 8)
    return {
        "teacher_hidden": draw_teacher_hidden(jax.random.fold_in(key_of[7], 71), 0),
        "teacher_gain": jnp.clip(1.0 + 0.1 * jax.random.normal(key_of[1], (DT,), jnp.float32), 0.5, 1.5).astype(jnp.bfloat16),
        "teacher_unembed": draw_teacher_unembed(jax.random.fold_in(key_of[7], 71), 0),
        "student_hidden": draw_student_hidden(jax.random.fold_in(key_of[7], 71), 0),
        "student_gain": jnp.clip(1.0 + 0.1 * jax.random.normal(key_of[4], (DS,), jnp.float32), 0.5, 1.5).astype(jnp.bfloat16),
        "student_unembed": draw_student_unembed(jax.random.fold_in(key_of[7], 71), 0),
        "labels": touch_ends(ranked_ids(key_of[6], (TOKENS,), VOCAB, 2), jax.random.fold_in(key_of[6], 3), 0, VOCAB - 1).astype(jnp.int32),
    }


SOFTEN_FACTOR = 2.0
DISTILL_FRACTION = 0.5
EPSILON = 1e-05

def rms_scale(values):
    return lax.rsqrt(lax.optimization_barrier(jnp.mean(values * values, axis=-1, keepdims=True)) + EPSILON)

def reference(teacher_hidden, teacher_gain, teacher_unembed, student_hidden, student_gain, student_unembed, labels):
    wide_teacher = teacher_hidden.astype(jnp.float32)
    normed_teacher = (wide_teacher * rms_scale(wide_teacher) * teacher_gain.astype(jnp.float32)).astype(jnp.bfloat16)
    wide_student = student_hidden.astype(jnp.float32)
    student_scale = rms_scale(wide_student)
    gain_student = student_gain.astype(jnp.float32)
    normed_student = (wide_student * student_scale * gain_student).astype(jnp.bfloat16)
    teacher_scores = jnp.dot(normed_teacher, teacher_unembed, preferred_element_type=jnp.float32)
    student_scores = jnp.dot(normed_student, student_unembed, preferred_element_type=jnp.float32)
    teacher_peak = lax.optimization_barrier(jnp.max(teacher_scores, axis=1, keepdims=True))
    student_peak = lax.optimization_barrier(jnp.max(student_scores, axis=1, keepdims=True))
    teacher_soft_probs = jnp.exp((teacher_scores - teacher_peak) / SOFTEN_FACTOR)
    student_soft_probs = jnp.exp((student_scores - student_peak) / SOFTEN_FACTOR)
    student_plain_probs = jnp.exp(student_scores - student_peak)
    teacher_partition_sum = lax.optimization_barrier(jnp.sum(teacher_soft_probs, axis=1, keepdims=True))
    student_partition_sum = lax.optimization_barrier(jnp.sum(student_soft_probs, axis=1, keepdims=True))
    plain_partition_sum = lax.optimization_barrier(jnp.sum(student_plain_probs, axis=1, keepdims=True))
    spanning_axis = lax.optimization_barrier(jnp.sum(teacher_soft_probs * (teacher_scores - student_scores), axis=1, keepdims=True))
    columns = jnp.arange(VOCAB, dtype=jnp.int32)
    label_logit_values = columns[None, :] == labels.astype(jnp.int32)[:, None]
    picked = lax.optimization_barrier(jnp.sum(jnp.where(label_logit_values, student_scores, 0.0), axis=1, keepdims=True))
    kl_divergence_term = spanning_axis / (SOFTEN_FACTOR * teacher_partition_sum) - (teacher_peak / SOFTEN_FACTOR + jnp.log(teacher_partition_sum)) + (student_peak / SOFTEN_FACTOR + jnp.log(student_partition_sum))
    label_loss_term = student_peak + jnp.log(plain_partition_sum) - picked
    per_token_loss = (DISTILL_FRACTION * SOFTEN_FACTOR ** 2 * kl_divergence_term + (1.0 - DISTILL_FRACTION) * label_loss_term)[:, 0]
    logit_gradient = (DISTILL_FRACTION * SOFTEN_FACTOR * (student_soft_probs / student_partition_sum - teacher_soft_probs / teacher_partition_sum) + (1.0 - DISTILL_FRACTION) * (student_plain_probs / plain_partition_sum - label_logit_values.astype(jnp.float32))).astype(jnp.bfloat16)
    weight_grad = lax.dot_general(normed_student, logit_gradient, (((0,), (0,)), ((), ())), preferred_element_type=jnp.float32).astype(jnp.bfloat16)
    normed_grad = lax.dot_general(logit_gradient, student_unembed, (((1,), (1,)), ((), ())), preferred_element_type=jnp.float32)
    scaled = normed_grad * gain_student
    inner_sum = lax.optimization_barrier(jnp.mean(scaled * wide_student, axis=1, keepdims=True))
    hidden_grad = student_scale * scaled - wide_student * student_scale ** 3 * inner_sum
    return (per_token_loss, hidden_grad, weight_grad)
```

```python
import jax
import jax.numpy as jnp
from jax import lax
from jax.sharding import Mesh, PartitionSpec as P

SOFTEN = 2.0
DISTILL = 0.5
EPSILON = 1e-05
SHRINK = 0.125
GROW = 8.0
XY = ("xl", "y")
DP = ("xl", "y", "c")
VOC = ("z", "xh")
ALL = DP + VOC
f32, bf16, f16 = jnp.float32, jnp.bfloat16, jnp.float16


def turn(n, k):
    return [(i, (i + k) % n) for i in range(n)]


def pick(a, i):
    return lax.dynamic_index_in_dim(a, i, 0, keepdims=False)


def spread(x, axes, n):
    return lax.all_to_all(
        jnp.broadcast_to(x[None], (n,) + x.shape), axes, split_axis=0, concat_axis=0, tiled=True
    )


def swap_core(x):
    return lax.ppermute(x, "c", turn(2, 1))


def in_order(mine, other, place):
    return jnp.where(place == 0, jnp.stack([mine, other]), jnp.stack([other, mine]))


def gather_z(x):
    z = lax.axis_index("z")
    half = x.shape[0] // 2
    ahead, behind = [x], [x]
    for _ in range(3):
        ahead.append(lax.ppermute(ahead[-1], "z", turn(8, 1)))
        behind.append(lax.ppermute(behind[-1], "z", turn(8, 7)))
    far = jnp.concatenate(
        [
            lax.ppermute(ahead[-1][:half], "z", turn(8, 1)),
            lax.ppermute(behind[-1][half:], "z", turn(8, 7)),
        ]
    )
    out = jnp.zeros((8,) + x.shape, x.dtype)
    for k, block in enumerate([x] + ahead[1:] + [far] + behind[:0:-1]):
        out = lax.dynamic_update_index_in_dim(out, block, (z - k) % 8, 0)
    return out


def sum_x(parts):
    x = lax.axis_index("xl")
    got = lax.ppermute((pick(parts, 1 - x) * SHRINK).astype(f16), "xl", turn(2, 1))
    return pick(parts, x) + got.astype(f32) * GROW


def sum_y(parts):
    y = lax.axis_index("y")
    total = pick(parts, y)
    for k in (1, 3, 2):
        got = lax.ppermute((pick(parts, (y + k) % 4) * SHRINK).astype(f16), "y", turn(4, k))
        total = total + got.astype(f32) * GROW
    return total


def scatter_xy(parts):
    n = parts.shape[-1]
    return sum_y(sum_x(parts.reshape(2, 384, n)).reshape(4, 96, n))


def scatter_yx(parts):
    n = parts.shape[-1]
    return sum_x(sum_y(parts.reshape(2, 4, 96, n).transpose(1, 0, 2, 3).reshape(4, 192, n)).reshape(2, 96, n))


def gather_x(block):
    got = lax.ppermute(block, "xl", turn(2, 1))
    return in_order(block, got, lax.axis_index("xl"))


def gather_y(block):
    y = lax.axis_index("y")
    out = jnp.zeros((4,) + block.shape, block.dtype)
    out = lax.dynamic_update_index_in_dim(out, block, y, 0)
    for k in (1, 3, 2):
        got = lax.ppermute(block, "y", turn(4, k))
        out = lax.dynamic_update_index_in_dim(out, got, (y - k) % 4, 0)
    return out


def gather_tokens(grad):
    left, right = grad[:, :1024], grad[:, 1024:]
    left = gather_y(gather_x(left)).transpose(1, 0, 2, 3).reshape(768, 1024)
    right = gather_x(gather_y(right)).reshape(768, 1024)
    return left, right


def dot(a, b):
    return jnp.dot(a, b, preferred_element_type=f32)


def per_device(t_hid, t_gain, t_un, s_hid, s_gain, s_un, labels):
    c = lax.axis_index("c")
    d = lax.axis_index(DP)
    v = lax.axis_index(VOC)

    def halves(w):
        mine = lax.dynamic_slice_in_dim(w, c * 2048, 2048, 1)
        theirs = lax.dynamic_slice_in_dim(w, (1 - c) * 2048, 2048, 1)
        return mine, swap_core(theirs)

    t_own, t_other = halves(t_un)
    s_own, s_other = halves(s_un)

    t_wide, s_wide = t_hid.astype(f32), s_hid.astype(f32)
    squares = jnp.stack([jnp.sum(t_wide * t_wide, axis=1), jnp.sum(s_wide * s_wide, axis=1)])
    squares = jnp.sum(spread(squares, VOC, 16), axis=0)
    scale_here = lax.rsqrt(squares / jnp.array([[16384.0], [4096.0]], f32) + EPSILON)
    scales = spread(scale_here, DP, 16).transpose(1, 0, 2).reshape(2, 768, 1)

    flip = [(a * 16 + b, b * 16 + a) for a in range(16) for b in range(16)]
    rows = lax.ppermute(jnp.concatenate([t_hid, s_hid], axis=1), ALL, flip)
    rows = in_order(rows, lax.ppermute(rows, "xh", turn(2, 1)), lax.axis_index("xh"))
    rows = gather_z(rows.reshape(96, 1280)).reshape(768, 1280)
    rows_other = swap_core(rows)

    def normed(raw, who):
        t_g = lax.dynamic_slice_in_dim(t_gain, who * 1024, 1024, 0).astype(f32)
        s_g = lax.dynamic_slice_in_dim(s_gain, who * 256, 256, 0).astype(f32)
        t = (raw[:, :1024].astype(f32) * scales[0] * t_g).astype(bf16)
        s = (raw[:, 1024:].astype(f32) * scales[1] * s_g).astype(bf16)
        return t, s

    other = d + 1 - 2 * c
    tn_own, sn_own = normed(rows, d)
    tn_other, sn_other = normed(rows_other, other)

    def logits(a_own, a_other, w_own, w_other):
        parts = [dot(a_own, w_own[:, k : k + 1024]) + dot(a_other, w_other[:, k : k + 1024]) for k in (0, 1024)]
        return jnp.concatenate([scatter_xy(parts[0]), scatter_yx(parts[1])], axis=1)

    t = logits(tn_own, tn_other, t_own, t_other)
    s = logits(sn_own, sn_other, s_own, s_other)

    wide_labels = labels.astype(f32)
    both_labels = in_order(wide_labels, swap_core(wide_labels), c).reshape(96).astype(jnp.int32)
    ids = v * 4096 + c * 2048 + jnp.arange(2048, dtype=jnp.int32)
    hit = ids[None, :] == both_labels[:, None]

    t_top, s_top = jnp.max(t, axis=1), jnp.max(s, axis=1)
    t_soft = jnp.exp((t - t_top[:, None]) / SOFTEN)
    stats = jnp.stack(
        [
            t_top,
            s_top,
            jnp.sum(t_soft, axis=1),
            jnp.sum(jnp.exp((s - s_top[:, None]) / SOFTEN), axis=1),
            jnp.sum(jnp.exp(s - s_top[:, None]), axis=1),
            jnp.sum(t_soft * (t - s), axis=1),
            jnp.sum(jnp.where(hit, s, 0.0), axis=1),
        ]
    )
    stats = jnp.stack([stats, swap_core(stats)])
    stats = spread(stats, VOC, 16).reshape(32, 7, 96)
    t_top, s_top = jnp.max(stats[:, 0], axis=0), jnp.max(stats[:, 1], axis=0)
    t_soften = jnp.exp((stats[:, 0] - t_top) / SOFTEN)
    s_soften = jnp.exp((stats[:, 1] - s_top) / SOFTEN)
    s_sharpen = jnp.exp(stats[:, 1] - s_top)
    t_total = jnp.sum(stats[:, 2] * t_soften, axis=0)
    s_total = jnp.sum(stats[:, 3] * s_soften, axis=0)
    sharp_total = jnp.sum(stats[:, 4] * s_sharpen, axis=0)
    across = jnp.sum(stats[:, 5] * t_soften, axis=0)
    picked = jnp.sum(stats[:, 6], axis=0)
    divergence = (
        across / (SOFTEN * t_total) - (t_top / SOFTEN + jnp.log(t_total)) + (s_top / SOFTEN + jnp.log(s_total))
    )
    loss = DISTILL * SOFTEN**2 * divergence + (1.0 - DISTILL) * (s_top + jnp.log(sharp_total) - picked)
    loss = pick(loss.reshape(2, 48), c)

    s_soft = jnp.exp((s - s_top[:, None]) / SOFTEN)
    t_soft = jnp.exp((t - t_top[:, None]) / SOFTEN)
    sharp = jnp.exp(s - s_top[:, None])
    grad = (
        DISTILL * SOFTEN * (s_soft / s_total[:, None] - t_soft / t_total[:, None])
        + (1.0 - DISTILL) * (sharp / sharp_total[:, None] - hit.astype(f32))
    ).astype(bf16)

    inner = jnp.sum(grad.astype(f32) * s, axis=1)
    inner = jnp.sum(spread(inner + swap_core(inner), VOC, 16), axis=0)
    inner = pick(inner.reshape(2, 48), c)

    left, right = gather_tokens(grad)

    def outer(a):
        over = (((0,), (0,)), ((), ()))
        return jnp.concatenate(
            [lax.dot_general(a, g, over, preferred_element_type=f32).astype(bf16) for g in (left, right)], axis=1
        )

    weight_own = outer(sn_own)
    weight_got = swap_core(outer(sn_other))
    weight_grad = in_order(weight_own, weight_got, c).transpose(1, 0, 2).reshape(256, 4096)

    def inward(w):
        over = (((1,), (1,)), ((), ()))
        return sum(
            lax.dot_general(g, w[:, k : k + 1024], over, preferred_element_type=f32)
            for g, k in ((left, 0), (right, 1024))
        )

    normed_grad = inward(s_own) + swap_core(inward(s_other))
    normed_grad = lax.all_to_all(
        normed_grad.reshape(16, 48, 256), VOC, split_axis=0, concat_axis=0, tiled=True
    )
    normed_grad = lax.ppermute(jnp.sum(normed_grad, axis=0), ALL, flip)
    scale = scale_here[1][:, None]
    gain = lax.dynamic_slice_in_dim(s_gain, v * 256, 256, 0).astype(f32)
    inner = inner[:, None] / (4096.0 * scale)
    hidden_grad = scale * (normed_grad * gain) - s_wide * scale**3 * inner
    return loss, hidden_grad, weight_grad


def solution(mesh):
    fine = Mesh(mesh.devices.reshape(2, 4, 2, 8, 2), ALL)
    both, rows = P(DP, VOC), P(DP)
    return jax.shard_map(
        per_device,
        mesh=fine,
        in_specs=(both, P(), both, both, P(), both, rows),
        out_specs=(rows, both, both),
        check_vma=False,
    )
```

```python
import jax
import jax.numpy as jnp
from jax import lax
from jax.sharding import Mesh, PartitionSpec as P

SOFTEN = 2.0
DISTILL = 0.5
EPSILON = 1e-05
SHRINK = 0.125
GROW = 8.0
XY = ("xl", "y")
DP = ("xl", "y", "c")
VOC = ("z", "xh")
ALL = DP + VOC
f32, bf16, f16 = jnp.float32, jnp.bfloat16, jnp.float16


def place_of(j, c, z, xh):
    return ((j * 2 + c) * 8 + z) * 2 + xh


PLACES = [(j, c, z, xh) for j in range(8) for c in range(2) for z in range(8) for xh in range(2)]
TO_PLANE = [(place_of(j, c, z, xh), place_of(j, c, (z + j) % 8, xh)) for j, c, z, xh in PLACES]
TO_COLUMN = [(place_of(j, c, z, xh), place_of((z - j) % 8, xh, z, c)) for j, c, z, xh in PLACES]


def back(pairs):
    return [(b, a) for a, b in pairs]


def turn(n, k):
    return [(i, (i + k) % n) for i in range(n)]


def pick(a, i):
    return lax.dynamic_index_in_dim(a, i, 0, keepdims=False)


def spread(x, axes, n):
    return lax.all_to_all(
        jnp.broadcast_to(x[None], (n,) + x.shape), axes, split_axis=0, concat_axis=0, tiled=True
    )


def hold(*values):
    return lax.optimization_barrier(values)


def swap_core(x):
    return lax.ppermute(x, "c", turn(2, 1))


def in_order(mine, other, place):
    return jnp.where(place == 0, jnp.stack([mine, other]), jnp.stack([other, mine]))


def shrink(x):
    return (x * SHRINK).astype(f16)


def grow(x):
    return x.astype(f32) * GROW


def ring(ahead, behind):
    return lax.ppermute(ahead, "z", turn(8, 1)), lax.ppermute(behind, "z", turn(8, 7))


def ring_end(ahead, behind):
    half = ahead.shape[0] // 2
    return jnp.concatenate(ring(ahead[:half], behind[half:]))


def in_z_order(blocks, place):
    out = jnp.zeros((8,) + blocks[0].shape, blocks[0].dtype)
    for k, block in enumerate(blocks):
        out = lax.dynamic_update_index_in_dim(out, block, (place - k) % 8, 0)
    return out


def from_x(x):
    return lax.ppermute(x, "xl", turn(2, 1))


def from_y(x, k):
    return lax.ppermute(x, "y", turn(4, k))


def dot(a, b):
    return jnp.dot(a, b, preferred_element_type=f32)


def softmax_sums(t, s, hit):
    t_top, s_top = jnp.max(t, axis=1), jnp.max(s, axis=1)
    t_soft = jnp.exp((t - t_top[:, None]) / SOFTEN)
    return jnp.stack(
        [
            t_top,
            s_top,
            jnp.sum(t_soft, axis=1),
            jnp.sum(jnp.exp((s - s_top[:, None]) / SOFTEN), axis=1),
            jnp.sum(jnp.exp(s - s_top[:, None]), axis=1),
            jnp.sum(t_soft * (t - s), axis=1),
            jnp.sum(jnp.where(hit, s, 0.0), axis=1),
        ]
    )


def common_sums(stats):
    t_top, s_top = jnp.max(stats[:, 0], axis=0), jnp.max(stats[:, 1], axis=0)
    t_soften = jnp.exp((stats[:, 0] - t_top) / SOFTEN)
    s_soften = jnp.exp((stats[:, 1] - s_top) / SOFTEN)
    s_sharpen = jnp.exp(stats[:, 1] - s_top)
    return (
        t_top,
        s_top,
        jnp.sum(stats[:, 2] * t_soften, axis=0),
        jnp.sum(stats[:, 3] * s_soften, axis=0),
        jnp.sum(stats[:, 4] * s_sharpen, axis=0),
        jnp.sum(stats[:, 5] * t_soften, axis=0),
        jnp.sum(stats[:, 6], axis=0),
    )


def all_stats(stats):
    stats = jnp.stack([stats, swap_core(stats)])
    return spread(stats, VOC, 16).reshape(32, 7, -1)


def loss_and_grad(t, s, hit, stats):
    t_top, s_top, t_total, s_total, sharp_total, across, picked = common_sums(stats)
    divergence = (
        across / (SOFTEN * t_total) - (t_top / SOFTEN + jnp.log(t_total)) + (s_top / SOFTEN + jnp.log(s_total))
    )
    loss = DISTILL * SOFTEN**2 * divergence + (1.0 - DISTILL) * (s_top + jnp.log(sharp_total) - picked)
    s_soft = jnp.exp((s - s_top[:, None]) / SOFTEN)
    t_soft = jnp.exp((t - t_top[:, None]) / SOFTEN)
    sharp = jnp.exp(s - s_top[:, None])
    grad = (
        DISTILL * SOFTEN * (s_soft / s_total[:, None] - t_soft / t_total[:, None])
        + (1.0 - DISTILL) * (sharp / sharp_total[:, None] - hit.astype(f32))
    ).astype(bf16)
    return loss, grad, jnp.sum(grad.astype(f32) * s, axis=1)


def per_device(t_hid, t_gain, t_un, s_hid, s_gain, s_un, labels):
    c = lax.axis_index("c")
    v = lax.axis_index(VOC)
    z = lax.axis_index("z")
    xh = lax.axis_index("xh")
    xl = lax.axis_index("xl")
    y = lax.axis_index("y")
    j = xl * 4 + y

    def columns(w, who):
        return lax.dynamic_slice_in_dim(w, who * 2048, 2048, 1)

    moved = lax.ppermute(jnp.concatenate([t_hid, s_hid], axis=1), ALL, TO_PLANE)
    t_wide, s_wide = t_hid.astype(f32), s_hid.astype(f32)
    squares = jnp.stack([jnp.sum(t_wide * t_wide, axis=1), jnp.sum(s_wide * s_wide, axis=1)])
    squares = spread(squares, VOC, 16)
    moved, squares = hold(moved, squares)
    scale = lax.rsqrt(jnp.sum(squares, axis=0) / jnp.array([[16384.0], [4096.0]], f32) + EPSILON)[:, :, None]
    f = (z - j) % 8 * 2 + xh
    t_g = lax.dynamic_slice_in_dim(t_gain, f * 1024, 1024, 0).astype(f32)
    s_g = lax.dynamic_slice_in_dim(s_gain, f * 256, 256, 0).astype(f32)
    block = jnp.concatenate(
        [
            (moved[:, :1024].astype(f32) * scale[0] * t_g).astype(bf16),
            (moved[:, 1024:].astype(f32) * scale[1] * s_g).astype(bf16),
        ],
        axis=1,
    )
    block = lax.ppermute(block, ALL, TO_COLUMN)
    block = in_order(block, lax.ppermute(block, "xh", turn(2, 1)), xh).reshape(96, 1280)

    a1, b1 = ring(block, block)
    a1, b1, t_un, s_un = hold(a1, b1, t_un, s_un)
    a2, b2 = ring(a1, b1)
    t_theirs, s_theirs = columns(t_un, 1 - c), columns(s_un, 1 - c)
    a2, b2, t_theirs, s_theirs = hold(a2, b2, t_theirs, s_theirs)
    t_other, s_other = swap_core(t_theirs), swap_core(s_theirs)
    t_own, s_own = columns(t_un, c), columns(s_un, c)
    a3, b3 = ring(a2, b2)
    blocks = [block, a1, a2, a3, ring_end(a3, b3), b3, b2, b1]
    tn = in_z_order([one[:, :1024] for one in blocks], z - j).reshape(768, 1024)
    sn = in_z_order([one[:, 1024:] for one in blocks], z - j).reshape(768, 256)
    tn_other, sn_other = swap_core(tn), swap_core(sn)

    def t_rows(rows, place):
        return pick(rows.reshape(2, 384, 1024), place)

    def s_rows(rows, place):
        return lax.dynamic_index_in_dim(rows.reshape(2, 4, 96, 256), place, 1, keepdims=False).reshape(192, 256)

    t_send = dot(t_rows(tn, 1 - xl), t_own)
    t_send, tn_other, sn_other = hold(t_send, tn_other, sn_other)
    t_send = shrink(t_send + dot(t_rows(tn_other, 1 - xl), t_other))
    t_got = from_x(t_send)
    sn, t_send = hold(sn, t_send)
    s_send = [
        shrink(dot(s_rows(sn, p), s_own) + dot(s_rows(sn_other, p), s_other)) for p in ((y + k) % 4 for k in (1, 3, 2))
    ]
    s_got = [from_y(part, k) for part, k in zip(s_send, (1, 3, 2))]
    tn, s_send = hold(tn, s_send)
    t_keep = dot(t_rows(tn, xl), t_own) + dot(t_rows(tn_other, xl), t_other)
    s_keep = dot(s_rows(sn, y), s_own) + dot(s_rows(sn_other, y), s_other)
    t_keep, s_keep, s_got = hold(t_keep, s_keep, s_got)
    s_keep = (s_keep + sum(grow(part) for part in s_got)).reshape(2, 96, 2048)
    s_got = from_x(shrink(pick(s_keep, 1 - xl)))
    t_keep = (t_keep + grow(t_got)).reshape(4, 96, 2048)
    t_got = [from_y(shrink(pick(t_keep, (y + k) % 4)), k) for k in (1, 3, 2)]
    s = pick(s_keep, xl) + grow(s_got)
    t = pick(t_keep, y) + sum(grow(part) for part in t_got)

    wide_labels = labels.astype(f32)
    wanted = in_order(wide_labels, swap_core(wide_labels), c).reshape(96).astype(jnp.int32)
    ids = v * 4096 + c * 2048 + jnp.arange(2048, dtype=jnp.int32)
    hit = ids[None, :] == wanted[:, None]
    loss, grad, inner = loss_and_grad(t, s, hit, all_stats(softmax_sums(t, s, hit)))
    loss = pick(loss.reshape(2, 48), c)

    left, right = grad[:, :1024], grad[:, 1024:]
    left_got = from_x(left)
    parts = [from_y(right, k) for k in (1, 2, 3)]
    left = in_order(left, left_got, xl)
    row = jnp.zeros((4, 96, 1024), bf16)
    for k, part in enumerate([right] + parts):
        row = lax.dynamic_update_index_in_dim(row, part, (y - k) % 4, 0)
    inner = inner + swap_core(inner)
    row, left, inner = hold(row, left, inner)
    right_got = from_x(row)
    parts = [from_y(left, k) for k in (1, 2, 3)]
    right = in_order(row, right_got, xl).reshape(768, 1024)

    over_columns = (((1,), (1,)), ((), ()))
    over_tokens = (((0,), (0,)), ((), ()))

    def inward(side, w):
        return lax.dot_general(side, w, over_columns, preferred_element_type=f32)

    def outer(rows, side):
        return lax.dot_general(rows, side, over_tokens, preferred_element_type=f32).astype(bf16)

    student = jnp.concatenate([sn, sn_other], axis=1)
    give, keep = inward(right, s_other[:, 1024:]), inward(right, s_own[:, 1024:])
    weight_right = outer(student, right)
    parts, give, keep, weight_right = hold(parts, give, keep, weight_right)
    out = jnp.zeros((2, 4, 96, 1024), bf16)
    for k, part in enumerate([left] + parts):
        out = lax.dynamic_update_index_in_dim(out, part, (y - k) % 4, 1)
    left = out.reshape(768, 1024)
    give = swap_core((give + inward(left, s_other[:, :1024])).astype(bf16))
    keep = keep + inward(left, s_own[:, :1024])
    normed_grad = (keep + give.astype(f32)).astype(bf16).reshape(8, 96, 256)
    normed_grad = lax.dynamic_slice_in_dim(jnp.concatenate([normed_grad, normed_grad]), 8 - j, 8, 0)
    inner = jnp.pad(inner, (0, 160)).astype(bf16)
    beside = jnp.broadcast_to(jnp.pad(inner[None], ((0, 7), (0, 0)))[None], (16, 8, 256))
    sums = jnp.concatenate([normed_grad.reshape(16, 48, 256), beside], axis=1)
    sums, left, student = hold(sums, left, student)
    sums = lax.all_to_all(sums, VOC, split_axis=0, concat_axis=0, tiled=True)
    weight = jnp.concatenate([outer(student, left), weight_right], axis=1)
    weight_own, weight_got = weight[:256], swap_core(weight[256:])
    weight_grad = jnp.concatenate(
        [jnp.where(c == 0, weight_own, weight_got), jnp.where(c == 0, weight_got, weight_own)], axis=1
    )
    sums, weight_grad = hold(sums, weight_grad)
    sums = jnp.sum(sums.astype(f32), axis=0)
    normed_grad = lax.ppermute(lax.ppermute(sums[:48], ALL, back(TO_COLUMN)), ALL, back(TO_PLANE))
    inner = pick(sums[48, :96].reshape(2, 48), c)[:, None] / (4096.0 * scale[1])
    s_g = lax.dynamic_slice_in_dim(s_gain, v * 256, 256, 0).astype(f32)
    hidden_grad = scale[1] * (normed_grad * s_g) - s_wide * scale[1] ** 3 * inner
    return loss, hidden_grad, weight_grad


def solution(mesh):
    fine = Mesh(mesh.devices.reshape(2, 4, 2, 8, 2), ALL)
    both, rows = P(DP, VOC), P(DP)
    return jax.shard_map(
        per_device,
        mesh=fine,
        in_specs=(both, P(), both, both, P(), both, rows),
        out_specs=(rows, both, both),
        check_vma=False,
    )
```

```python
import jax
import jax.numpy as jnp
from jax import lax
from jax.sharding import Mesh, PartitionSpec as P

SOFTEN = 2.0
DISTILL = 0.5
EPSILON = 1e-05
SHRINK = 0.125
GROW = 8.0
XY = ("xl", "y")
DP = ("xl", "y", "c")
VOC = ("z", "xh")
ALL = DP + VOC
f32, bf16, f16 = jnp.float32, jnp.bfloat16, jnp.float16


def place_of(j, c, z, xh):
    return ((j * 2 + c) * 8 + z) * 2 + xh


PLACES = [(j, c, z, xh) for j in range(8) for c in range(2) for z in range(8) for xh in range(2)]
TO_PLANE = [(place_of(j, c, z, xh), place_of(j, c, (z + j) % 8, xh)) for j, c, z, xh in PLACES]
TO_COLUMN = [(place_of(j, c, z, xh), place_of((z - j) % 8, xh, z, c)) for j, c, z, xh in PLACES]


def back(pairs):
    return [(b, a) for a, b in pairs]


def turn(n, k):
    return [(i, (i + k) % n) for i in range(n)]


def pick(a, i):
    return lax.dynamic_index_in_dim(a, i, 0, keepdims=False)


def spread(x, axes, n):
    return lax.all_to_all(
        jnp.broadcast_to(x[None], (n,) + x.shape), axes, split_axis=0, concat_axis=0, tiled=True
    )


def hold(*values):
    return lax.optimization_barrier(values)


def swap_core(x):
    return lax.ppermute(x, "c", turn(2, 1))


def in_order(mine, other, place):
    return jnp.where(place == 0, jnp.stack([mine, other]), jnp.stack([other, mine]))


def shrink(x):
    return (x * SHRINK).astype(f16)


def grow(x):
    return x.astype(f32) * GROW


def ring(ahead, behind):
    return lax.ppermute(ahead, "z", turn(8, 1)), lax.ppermute(behind, "z", turn(8, 7))


def ring_end(ahead, behind):
    half = ahead.shape[0] // 2
    return jnp.concatenate(ring(ahead[:half], behind[half:]))


def in_z_order(blocks, place):
    out = jnp.zeros((8,) + blocks[0].shape, blocks[0].dtype)
    for k, block in enumerate(blocks):
        out = lax.dynamic_update_index_in_dim(out, block, (place - k) % 8, 0)
    return out


def from_x(x):
    return lax.ppermute(x, "xl", turn(2, 1))


def from_y(x, k):
    return lax.ppermute(x, "y", turn(4, k))


def dot(a, b):
    return jnp.dot(a, b, preferred_element_type=f32)


def softmax_sums(t, s, hit):
    t_top, s_top = jnp.max(t, axis=1), jnp.max(s, axis=1)
    t_soft = jnp.exp((t - t_top[:, None]) / SOFTEN)
    return jnp.stack(
        [
            t_top,
            s_top,
            jnp.sum(t_soft, axis=1),
            jnp.sum(jnp.exp((s - s_top[:, None]) / SOFTEN), axis=1),
            jnp.sum(jnp.exp(s - s_top[:, None]), axis=1),
            jnp.sum(t_soft * (t - s), axis=1),
            jnp.sum(jnp.where(hit, s, 0.0), axis=1),
        ]
    )


def common_sums(stats):
    t_top, s_top = jnp.max(stats[:, 0], axis=0), jnp.max(stats[:, 1], axis=0)
    t_soften = jnp.exp((stats[:, 0] - t_top) / SOFTEN)
    s_soften = jnp.exp((stats[:, 1] - s_top) / SOFTEN)
    s_sharpen = jnp.exp(stats[:, 1] - s_top)
    return (
        t_top,
        s_top,
        jnp.sum(stats[:, 2] * t_soften, axis=0),
        jnp.sum(stats[:, 3] * s_soften, axis=0),
        jnp.sum(stats[:, 4] * s_sharpen, axis=0),
        jnp.sum(stats[:, 5] * t_soften, axis=0),
        jnp.sum(stats[:, 6], axis=0),
    )


def all_stats(stats):
    stats = jnp.stack([stats, swap_core(stats)])
    return spread(stats, VOC, 16).reshape(32, 7, -1)


def loss_and_grad(t, s, hit, stats):
    t_top, s_top, t_total, s_total, sharp_total, across, picked = common_sums(stats)
    divergence = (
        across / (SOFTEN * t_total) - (t_top / SOFTEN + jnp.log(t_total)) + (s_top / SOFTEN + jnp.log(s_total))
    )
    loss = DISTILL * SOFTEN**2 * divergence + (1.0 - DISTILL) * (s_top + jnp.log(sharp_total) - picked)
    s_soft = jnp.exp((s - s_top[:, None]) / SOFTEN)
    t_soft = jnp.exp((t - t_top[:, None]) / SOFTEN)
    sharp = jnp.exp(s - s_top[:, None])
    grad = (
        DISTILL * SOFTEN * (s_soft / s_total[:, None] - t_soft / t_total[:, None])
        + (1.0 - DISTILL) * (sharp / sharp_total[:, None] - hit.astype(f32))
    ).astype(bf16)
    return loss, grad, jnp.sum(grad.astype(f32) * s, axis=1)


def per_device(t_hid, t_gain, t_un, s_hid, s_gain, s_un, labels):
    c = lax.axis_index("c")
    v = lax.axis_index(VOC)
    z = lax.axis_index("z")
    xh = lax.axis_index("xh")
    xl = lax.axis_index("xl")
    y = lax.axis_index("y")
    j = xl * 4 + y

    def columns(w, who):
        return lax.dynamic_slice_in_dim(w, who * 2048, 2048, 1)

    moved = lax.ppermute(jnp.concatenate([t_hid, s_hid], axis=1), ALL, TO_PLANE)
    t_wide, s_wide = t_hid.astype(f32), s_hid.astype(f32)
    squares = jnp.stack([jnp.sum(t_wide * t_wide, axis=1), jnp.sum(s_wide * s_wide, axis=1)])
    squares = spread(squares, VOC, 16)
    moved, squares, t_theirs, s_theirs = hold(moved, squares, columns(t_un, 1 - c), columns(s_un, 1 - c))
    t_other, s_other = swap_core(t_theirs), swap_core(s_theirs)
    t_own, s_own = columns(t_un, c), columns(s_un, c)
    scale = lax.rsqrt(jnp.sum(squares, axis=0) / jnp.array([[16384.0], [4096.0]], f32) + EPSILON)[:, :, None]
    f = (z - j) % 8 * 2 + xh
    t_g = lax.dynamic_slice_in_dim(t_gain, f * 1024, 1024, 0).astype(f32)
    s_g = lax.dynamic_slice_in_dim(s_gain, f * 256, 256, 0).astype(f32)
    block = jnp.concatenate(
        [
            (moved[:, :1024].astype(f32) * scale[0] * t_g).astype(bf16),
            (moved[:, 1024:].astype(f32) * scale[1] * s_g).astype(bf16),
        ],
        axis=1,
    )
    block = lax.ppermute(block, ALL, TO_COLUMN)
    block = in_order(block, lax.ppermute(block, "xh", turn(2, 1)), xh).reshape(96, 1280)

    a1, b1 = ring(block, block)
    a2, b2 = ring(a1, b1)
    a3, b3 = ring(a2, b2)
    blocks = [block, a1, a2, a3, ring_end(a3, b3), b3, b2, b1]
    tn = in_z_order([one[:, :1024] for one in blocks], z - j).reshape(768, 1024)
    sn = in_z_order([one[:, 1024:] for one in blocks], z - j).reshape(768, 256)
    tn_other, sn_other = swap_core(tn), swap_core(sn)

    def t_rows(rows, place):
        return pick(rows.reshape(2, 384, 1024), place)

    def s_rows(rows, place):
        return lax.dynamic_index_in_dim(rows.reshape(2, 4, 96, 256), place, 1, keepdims=False).reshape(192, 256)

    s_send = [
        shrink(dot(s_rows(sn, p), s_own) + dot(s_rows(sn_other, p), s_other)) for p in ((y + k) % 4 for k in (1, 3, 2))
    ]
    s_got = [from_y(part, k) for part, k in zip(s_send, (1, 3, 2))]
    tn, s_send = hold(tn, s_send)
    t_send = shrink(dot(t_rows(tn, 1 - xl), t_own) + dot(t_rows(tn_other, 1 - xl), t_other))
    t_got = from_x(t_send)
    tn, t_send = hold(tn, t_send)
    t_keep = dot(t_rows(tn, xl), t_own) + dot(t_rows(tn_other, xl), t_other)
    s_keep = dot(s_rows(sn, y), s_own) + dot(s_rows(sn_other, y), s_other)
    t_keep, s_keep, s_got = hold(t_keep, s_keep, s_got)
    s_keep = (s_keep + sum(grow(part) for part in s_got)).reshape(2, 96, 2048)
    s_got = from_x(shrink(pick(s_keep, 1 - xl)))
    t_keep = (t_keep + grow(t_got)).reshape(4, 96, 2048)
    t_got = [from_y(shrink(pick(t_keep, (y + k) % 4)), k) for k in (1, 3, 2)]
    s = pick(s_keep, xl) + grow(s_got)
    t = pick(t_keep, y) + sum(grow(part) for part in t_got)

    wide_labels = labels.astype(f32)
    wanted = in_order(wide_labels, swap_core(wide_labels), c).reshape(96).astype(jnp.int32)
    ids = v * 4096 + c * 2048 + jnp.arange(2048, dtype=jnp.int32)
    hit = ids[None, :] == wanted[:, None]
    loss, grad, inner = loss_and_grad(t, s, hit, all_stats(softmax_sums(t, s, hit)))
    loss = pick(loss.reshape(2, 48), c)

    left, right = grad[:, :1024], grad[:, 1024:]
    left_got = from_x(left)
    parts = [from_y(right, k) for k in (1, 2, 3)]
    left = in_order(left, left_got, xl)
    row = jnp.zeros((4, 96, 1024), bf16)
    for k, part in enumerate([right] + parts):
        row = lax.dynamic_update_index_in_dim(row, part, (y - k) % 4, 0)
    inner = inner + swap_core(inner)
    row, left, inner = hold(row, left, inner)
    right_got = from_x(row)
    parts = [from_y(left, k) for k in (1, 2, 3)]
    right = in_order(row, right_got, xl).reshape(768, 1024)

    over_columns = (((1,), (1,)), ((), ()))
    over_tokens = (((0,), (0,)), ((), ()))

    def inward(side, w):
        return lax.dot_general(side, w, over_columns, preferred_element_type=f32)

    def outer(rows, side):
        return lax.dot_general(rows, side, over_tokens, preferred_element_type=f32).astype(bf16)

    student = jnp.concatenate([sn, sn_other], axis=1)
    give, keep = inward(right, s_other[:, 1024:]), inward(right, s_own[:, 1024:])
    parts, give, keep = hold(parts, give, keep)
    out = jnp.zeros((2, 4, 96, 1024), bf16)
    for k, part in enumerate([left] + parts):
        out = lax.dynamic_update_index_in_dim(out, part, (y - k) % 4, 1)
    left = out.reshape(768, 1024)
    give = swap_core((give + inward(left, s_other[:, :1024])).astype(bf16))
    keep = keep + inward(left, s_own[:, :1024])
    normed_grad = (keep + give.astype(f32)).astype(bf16).reshape(8, 96, 256)
    normed_grad = lax.dynamic_slice_in_dim(jnp.concatenate([normed_grad, normed_grad]), 8 - j, 8, 0)
    inner = jnp.pad(inner, (0, 160)).astype(bf16)
    beside = jnp.broadcast_to(jnp.pad(inner[None], ((0, 7), (0, 0)))[None], (16, 8, 256))
    sums = jnp.concatenate([normed_grad.reshape(16, 48, 256), beside], axis=1)
    sums = lax.all_to_all(sums, VOC, split_axis=0, concat_axis=0, tiled=True)
    weight = jnp.concatenate([outer(student, left), outer(student, right)], axis=1)
    weight_own, weight_got = weight[:256], swap_core(weight[256:])
    weight_grad = jnp.concatenate(
        [jnp.where(c == 0, weight_own, weight_got), jnp.where(c == 0, weight_got, weight_own)], axis=1
    )
    sums, weight_grad = hold(sums, weight_grad)
    sums = jnp.sum(sums.astype(f32), axis=0)
    normed_grad = lax.ppermute(lax.ppermute(sums[:48], ALL, back(TO_COLUMN)), ALL, back(TO_PLANE))
    inner = pick(sums[48, :96].reshape(2, 48), c)[:, None] / (4096.0 * scale[1])
    s_g = lax.dynamic_slice_in_dim(s_gain, v * 256, 256, 0).astype(f32)
    hidden_grad = scale[1] * (normed_grad * s_g) - s_wide * scale[1] ** 3 * inner
    return loss, hidden_grad, weight_grad


def solution(mesh):
    fine = Mesh(mesh.devices.reshape(2, 4, 2, 8, 2), ALL)
    both, rows = P(DP, VOC), P(DP)
    return jax.shard_map(
        per_device,
        mesh=fine,
        in_specs=(both, P(), both, both, P(), both, rows),
        out_specs=(rows, both, both),
        check_vma=False,
    )
```

```python
import jax
import jax.numpy as jnp
from jax import lax
from jax.sharding import Mesh, PartitionSpec as P

SOFTEN = 2.0
DISTILL = 0.5
EPSILON = 1e-05
SHRINK = 0.125
GROW = 8.0
XY = ("xl", "y")
DP = ("xl", "y", "c")
VOC = ("z", "xh")
ALL = DP + VOC
f32, bf16, f16 = jnp.float32, jnp.bfloat16, jnp.float16


def place_of(j, c, z, xh):
    return ((j * 2 + c) * 8 + z) * 2 + xh


PLACES = [(j, c, z, xh) for j in range(8) for c in range(2) for z in range(8) for xh in range(2)]


def apart(j, z):
    return ((z // 4) ^ (j // 4)) * 4 + (z - j) % 4


def beside(j, z):
    return ((z // 4) ^ (j // 4)) * 4 + (z + j) % 4


TO_PLANE = [(place_of(j, c, z, xh), place_of(j, c, apart(j, z), xh)) for j, c, z, xh in PLACES]
TO_COLUMN = [(place_of(j, c, z, xh), place_of(beside(j, z), xh, z, c)) for j, c, z, xh in PLACES]
TO_NEXT = [(place_of(j, c, z, xh), place_of(beside(j, z), xh, z, 1 - c)) for j, c, z, xh in PLACES]


def back(pairs):
    return [(b, a) for a, b in pairs]


def turn(n, k):
    return [(i, (i + k) % n) for i in range(n)]


def pick(a, i):
    return lax.dynamic_index_in_dim(a, i, 0, keepdims=False)


def spread(x, axes, n):
    return lax.all_to_all(
        jnp.broadcast_to(x[None], (n,) + x.shape), axes, split_axis=0, concat_axis=0, tiled=True
    )


def hold(*values):
    return lax.optimization_barrier(values)


def swap_core(x):
    return lax.ppermute(x, "c", turn(2, 1))


def in_order(mine, other, place):
    return jnp.where(place == 0, jnp.stack([mine, other]), jnp.stack([other, mine]))


def shrink(x):
    return (x * SHRINK).astype(f16)


def grow(x):
    return x.astype(f32) * GROW


def ring(ahead, behind):
    return lax.ppermute(ahead, "z", turn(8, 1)), lax.ppermute(behind, "z", turn(8, 7))


def ring_end(ahead, behind):
    half = ahead.shape[0] // 2
    return jnp.concatenate(ring(ahead[:half], behind[half:]))


def in_z_order(blocks, place):
    out = jnp.zeros((8,) + blocks[0].shape, blocks[0].dtype)
    for k, block in enumerate(blocks):
        out = lax.dynamic_update_index_in_dim(out, block, (place - k) % 8, 0)
    return out


def from_x(x):
    return lax.ppermute(x, "xl", turn(2, 1))


def from_y(x, k):
    return lax.ppermute(x, "y", turn(4, k))


def dot(a, b):
    return jnp.dot(a, b, preferred_element_type=f32)


def softmax_sums(t, s, hit):
    t_top, s_top = jnp.max(t, axis=1), jnp.max(s, axis=1)
    t_soft = jnp.exp((t - t_top[:, None]) / SOFTEN)
    return jnp.stack(
        [
            t_top,
            s_top,
            jnp.sum(t_soft, axis=1),
            jnp.sum(jnp.exp((s - s_top[:, None]) / SOFTEN), axis=1),
            jnp.sum(jnp.exp(s - s_top[:, None]), axis=1),
            jnp.sum(t_soft * (t - s), axis=1),
            jnp.sum(jnp.where(hit, s, 0.0), axis=1),
        ]
    )


def common_sums(stats):
    t_top, s_top = jnp.max(stats[:, 0], axis=0), jnp.max(stats[:, 1], axis=0)
    t_soften = jnp.exp((stats[:, 0] - t_top) / SOFTEN)
    s_soften = jnp.exp((stats[:, 1] - s_top) / SOFTEN)
    s_sharpen = jnp.exp(stats[:, 1] - s_top)
    return (
        t_top,
        s_top,
        jnp.sum(stats[:, 2] * t_soften, axis=0),
        jnp.sum(stats[:, 3] * s_soften, axis=0),
        jnp.sum(stats[:, 4] * s_sharpen, axis=0),
        jnp.sum(stats[:, 5] * t_soften, axis=0),
        jnp.sum(stats[:, 6], axis=0),
    )


def all_stats(stats):
    stats = jnp.stack([stats, swap_core(stats)])
    return spread(stats, VOC, 16).reshape(32, 7, -1)


def loss_and_grad(t, s, hit, stats):
    t_top, s_top, t_total, s_total, sharp_total, across, picked = common_sums(stats)
    divergence = (
        across / (SOFTEN * t_total) - (t_top / SOFTEN + jnp.log(t_total)) + (s_top / SOFTEN + jnp.log(s_total))
    )
    loss = DISTILL * SOFTEN**2 * divergence + (1.0 - DISTILL) * (s_top + jnp.log(sharp_total) - picked)
    s_soft = jnp.exp((s - s_top[:, None]) / SOFTEN)
    t_soft = jnp.exp((t - t_top[:, None]) / SOFTEN)
    sharp = jnp.exp(s - s_top[:, None])
    grad = (
        DISTILL * SOFTEN * (s_soft / s_total[:, None] - t_soft / t_total[:, None])
        + (1.0 - DISTILL) * (sharp / sharp_total[:, None] - hit.astype(f32))
    ).astype(bf16)
    return loss, grad, jnp.sum(grad.astype(f32) * s, axis=1)


def per_device(t_hid, t_gain, t_un, s_hid, s_gain, s_un, labels):
    c = lax.axis_index("c")
    v = lax.axis_index(VOC)
    z = lax.axis_index("z")
    xh = lax.axis_index("xh")
    xl = lax.axis_index("xl")
    y = lax.axis_index("y")

    def columns(w, who):
        return lax.dynamic_slice_in_dim(w, who * 2048, 2048, 1)

    moved = lax.ppermute(jnp.concatenate([t_hid, s_hid], axis=1), ALL, TO_PLANE)
    t_wide, s_wide = t_hid.astype(f32), s_hid.astype(f32)
    squares = jnp.stack([jnp.sum(t_wide * t_wide, axis=1), jnp.sum(s_wide * s_wide, axis=1)])
    squares = spread(squares, VOC, 16)
    moved, squares, t_theirs, s_theirs = hold(moved, squares, columns(t_un, 1 - c), columns(s_un, 1 - c))
    t_other, s_other = swap_core(t_theirs), swap_core(s_theirs)
    t_own, s_own = columns(t_un, c), columns(s_un, c)
    scale = lax.rsqrt(jnp.sum(squares, axis=0) / jnp.array([[16384.0], [4096.0]], f32) + EPSILON)[:, :, None]
    f = (((z // 4) ^ xl) * 4 + (z + y) % 4) * 2 + xh
    t_g = lax.dynamic_slice_in_dim(t_gain, f * 1024, 1024, 0).astype(f32)
    s_g = lax.dynamic_slice_in_dim(s_gain, f * 256, 256, 0).astype(f32)
    block = jnp.concatenate(
        [
            (moved[:, :1024].astype(f32) * scale[0] * t_g).astype(bf16),
            (moved[:, 1024:].astype(f32) * scale[1] * s_g).astype(bf16),
        ],
        axis=1,
    )
    block = in_order(lax.ppermute(block, ALL, TO_COLUMN), lax.ppermute(block, ALL, TO_NEXT), xh).reshape(96, 1280)

    a1, b1 = ring(block, block)
    a2, b2 = ring(a1, b1)
    a3, b3 = ring(a2, b2)
    blocks = [block, a1, a2, a3, ring_end(a3, b3), b3, b2, b1]
    tn = in_z_order([one[:, :1024] for one in blocks], z).reshape(768, 1024)
    sn = in_z_order([one[:, 1024:] for one in blocks], z).reshape(768, 256)
    tn_other, sn_other = swap_core(tn), swap_core(sn)

    def s_rows(q):
        own, other = (rows.reshape(2, 4, 96, 256)[:, q].reshape(192, 256) for rows in (sn, sn_other))
        return dot(own, s_own) + dot(other, s_other)

    s_send = [shrink(s_rows(4 - k)) for k in (1, 3)]
    s_got = [from_y(part, k) for part, k in zip(s_send, (1, 3))]
    tn, s_send = hold(tn, s_send)
    t_send = shrink(dot(tn[384:], t_own) + dot(tn_other[384:], t_other))
    t_got = from_x(t_send)
    sn, t_send = hold(sn, t_send)
    s_send = shrink(s_rows(2))
    s_got.append(from_y(s_send, 2))
    tn, sn, s_send = hold(tn, sn, s_send)
    t_keep = dot(tn[:384], t_own) + dot(tn_other[:384], t_other)
    s_keep = s_rows(0)
    t_keep, s_keep, s_got = hold(t_keep, s_keep, s_got)
    s_keep = (s_keep + sum(grow(part) for part in s_got)).reshape(2, 96, 2048)
    s_got = from_x(shrink(s_keep[1]))
    t_keep = (t_keep + grow(t_got)).reshape(4, 96, 2048)
    t_got = [from_y(shrink(t_keep[4 - k]), k) for k in (1, 3, 2)]
    s = s_keep[0] + grow(s_got)
    t = t_keep[0] + sum(grow(part) for part in t_got)

    wide_labels = labels.astype(f32)
    wanted = in_order(wide_labels, swap_core(wide_labels), c).reshape(96).astype(jnp.int32)
    ids = v * 4096 + c * 2048 + jnp.arange(2048, dtype=jnp.int32)
    hit = ids[None, :] == wanted[:, None]
    loss, grad, inner = loss_and_grad(t, s, hit, all_stats(softmax_sums(t, s, hit)))
    loss = pick(loss.reshape(2, 48), c)

    left, right = grad[:, :1024], grad[:, 1024:]
    left_got, right_got = from_x(left), from_x(right)
    far = jnp.concatenate([from_y(right, k) for k in (1, 2, 3)])
    pair = jnp.concatenate([left, left_got])
    pairs = [pair] + [from_y(pair, k) for k in (1, 2, 3)]
    right = jnp.concatenate([right, far, right_got, from_x(far)])
    inner = inner + swap_core(inner)

    over_columns = (((1,), (1,)), ((), ()))
    over_tokens = (((0,), (0,)), ((), ()))

    def inward(side, w):
        return lax.dot_general(side, w, over_columns, preferred_element_type=f32)

    def outer(rows, side):
        return lax.dot_general(rows, side, over_tokens, preferred_element_type=f32).astype(bf16)

    student = jnp.concatenate([sn, sn_other], axis=1)
    give, keep = inward(right, s_other[:, 1024:]), inward(right, s_own[:, 1024:])
    pairs, give, keep, inner = hold(pairs, give, keep, inner)
    left = jnp.concatenate([one[:96] for one in pairs] + [one[96:] for one in pairs])
    give = swap_core((give + inward(left, s_other[:, :1024])).astype(bf16))
    keep = keep + inward(left, s_own[:, :1024])
    normed_grad = (keep + give.astype(f32)).astype(bf16)
    inner = jnp.pad(inner, (0, 160)).astype(bf16)
    beside = jnp.broadcast_to(jnp.pad(inner[None], ((0, 7), (0, 0)))[None], (16, 8, 256))
    sums = jnp.concatenate([normed_grad.reshape(16, 48, 256), beside], axis=1)
    sums = lax.all_to_all(sums, VOC, split_axis=0, concat_axis=0, tiled=True)
    weight = jnp.concatenate([outer(student, left), outer(student, right)], axis=1)
    weight_own, weight_got = weight[:256], swap_core(weight[256:])
    weight_grad = jnp.concatenate(
        [jnp.where(c == 0, weight_own, weight_got), jnp.where(c == 0, weight_got, weight_own)], axis=1
    )
    sums, weight_grad = hold(sums, weight_grad)
    sums = jnp.sum(sums.astype(f32), axis=0)
    normed_grad = lax.ppermute(lax.ppermute(sums[:48], ALL, back(TO_COLUMN)), ALL, back(TO_PLANE))
    inner = pick(sums[48, :96].reshape(2, 48), c)[:, None] / (4096.0 * scale[1])
    s_g = lax.dynamic_slice_in_dim(s_gain, v * 256, 256, 0).astype(f32)
    hidden_grad = scale[1] * (normed_grad * s_g) - s_wide * scale[1] ** 3 * inner
    return loss, hidden_grad, weight_grad


def solution(mesh):
    fine = Mesh(mesh.devices.reshape(2, 4, 2, 8, 2), ALL)
    both, rows = P(DP, VOC), P(DP)
    return jax.shard_map(
        per_device,
        mesh=fine,
        in_specs=(both, P(), both, both, P(), both, rows),
        out_specs=(rows, both, both),
        check_vma=False,
    )
```

```python
import jax
import jax.numpy as jnp
from jax import lax
from jax.sharding import Mesh, PartitionSpec as P

SOFTEN = 2.0
DISTILL = 0.5
EPSILON = 1e-05
SHRINK = 0.125
GROW = 8.0
XY = ("xl", "y")
DP = ("xl", "y", "c")
VOC = ("z", "xh")
ALL = DP + VOC
f32, bf16, f16 = jnp.float32, jnp.bfloat16, jnp.float16


def place_of(j, c, z, xh):
    return ((j * 2 + c) * 8 + z) * 2 + xh


PLACES = [(j, c, z, xh) for j in range(8) for c in range(2) for z in range(8) for xh in range(2)]


def apart(j, z):
    return ((z // 4) ^ (j // 4)) * 4 + (z - j) % 4


def beside(j, z):
    return ((z // 4) ^ (j // 4)) * 4 + (z + j) % 4


TO_PLANE = [(place_of(j, c, z, xh), place_of(j, c, apart(j, z), xh)) for j, c, z, xh in PLACES]
TO_COLUMN = [(place_of(j, c, z, xh), place_of(beside(j, z), xh, z, c)) for j, c, z, xh in PLACES]
TO_NEXT = [(place_of(j, c, z, xh), place_of(beside(j, z), xh, z, 1 - c)) for j, c, z, xh in PLACES]


def back(pairs):
    return [(b, a) for a, b in pairs]


def turn(n, k):
    return [(i, (i + k) % n) for i in range(n)]


def pick(a, i):
    return lax.dynamic_index_in_dim(a, i, 0, keepdims=False)


def spread(x, axes, n):
    return lax.all_to_all(
        jnp.broadcast_to(x[None], (n,) + x.shape), axes, split_axis=0, concat_axis=0, tiled=True
    )


def hold(*values):
    return lax.optimization_barrier(values)


def swap_core(x):
    return lax.ppermute(x, "c", turn(2, 1))


def in_order(mine, other, place):
    return jnp.where(place == 0, jnp.stack([mine, other]), jnp.stack([other, mine]))


def shrink(x):
    return (x * SHRINK).astype(f16)


def grow(x):
    return x.astype(f32) * GROW


def ring(ahead, behind):
    return lax.ppermute(ahead, "z", turn(8, 1)), lax.ppermute(behind, "z", turn(8, 7))


def ring_end(ahead, behind):
    half = ahead.shape[0] // 2
    return jnp.concatenate(ring(ahead[:half], behind[half:]))


def in_z_order(blocks, place):
    out = jnp.zeros((8,) + blocks[0].shape, blocks[0].dtype)
    for k, block in enumerate(blocks):
        out = lax.dynamic_update_index_in_dim(out, block, (place - k) % 8, 0)
    return out


def from_x(x):
    return lax.ppermute(x, "xl", turn(2, 1))


def from_y(x, k):
    return lax.ppermute(x, "y", turn(4, k))


def dot(a, b):
    return jnp.dot(a, b, preferred_element_type=f32)


def softmax_sums(t, s, hit):
    t_top, s_top = jnp.max(t, axis=1), jnp.max(s, axis=1)
    t_soft = jnp.exp((t - t_top[:, None]) / SOFTEN)
    return jnp.stack(
        [
            t_top,
            s_top,
            jnp.sum(t_soft, axis=1),
            jnp.sum(jnp.exp((s - s_top[:, None]) / SOFTEN), axis=1),
            jnp.sum(jnp.exp(s - s_top[:, None]), axis=1),
            jnp.sum(t_soft * (t - s), axis=1),
            jnp.sum(jnp.where(hit, s, 0.0), axis=1),
        ]
    )


def common_sums(stats):
    t_top, s_top = jnp.max(stats[:, 0], axis=0), jnp.max(stats[:, 1], axis=0)
    t_soften = jnp.exp((stats[:, 0] - t_top) / SOFTEN)
    s_soften = jnp.exp((stats[:, 1] - s_top) / SOFTEN)
    s_sharpen = jnp.exp(stats[:, 1] - s_top)
    return (
        t_top,
        s_top,
        jnp.sum(stats[:, 2] * t_soften, axis=0),
        jnp.sum(stats[:, 3] * s_soften, axis=0),
        jnp.sum(stats[:, 4] * s_sharpen, axis=0),
        jnp.sum(stats[:, 5] * t_soften, axis=0),
        jnp.sum(stats[:, 6], axis=0),
    )


def all_stats(stats):
    stats = jnp.stack([stats, swap_core(stats)])
    return spread(stats, VOC, 16).reshape(32, 7, -1)


def loss_and_grad(t, s, hit, stats):
    t_top, s_top, t_total, s_total, sharp_total, across, picked = common_sums(stats)
    divergence = (
        across / (SOFTEN * t_total) - (t_top / SOFTEN + jnp.log(t_total)) + (s_top / SOFTEN + jnp.log(s_total))
    )
    loss = DISTILL * SOFTEN**2 * divergence + (1.0 - DISTILL) * (s_top + jnp.log(sharp_total) - picked)
    s_soft = jnp.exp((s - s_top[:, None]) / SOFTEN)
    t_soft = jnp.exp((t - t_top[:, None]) / SOFTEN)
    sharp = jnp.exp(s - s_top[:, None])
    grad = (
        DISTILL * SOFTEN * (s_soft / s_total[:, None] - t_soft / t_total[:, None])
        + (1.0 - DISTILL) * (sharp / sharp_total[:, None] - hit.astype(f32))
    ).astype(bf16)
    return loss, grad, jnp.sum(grad.astype(f32) * s, axis=1)


def per_device(t_hid, t_gain, t_un, s_hid, s_gain, s_un, labels):
    c = lax.axis_index("c")
    v = lax.axis_index(VOC)
    z = lax.axis_index("z")
    xh = lax.axis_index("xh")
    xl = lax.axis_index("xl")
    y = lax.axis_index("y")

    def columns(w, who):
        return lax.dynamic_slice_in_dim(w, who * 2048, 2048, 1)

    moved = lax.ppermute(jnp.concatenate([t_hid, s_hid], axis=1), ALL, TO_PLANE)
    t_wide, s_wide = t_hid.astype(f32), s_hid.astype(f32)
    squares = jnp.stack([jnp.sum(t_wide * t_wide, axis=1), jnp.sum(s_wide * s_wide, axis=1)])
    squares = spread(squares, VOC, 16)
    moved, squares, t_theirs, s_theirs = hold(moved, squares, columns(t_un, 1 - c), columns(s_un, 1 - c))
    t_other, s_other = swap_core(t_theirs), swap_core(s_theirs)
    t_own, s_own = columns(t_un, c), columns(s_un, c)
    scale = lax.rsqrt(jnp.sum(squares, axis=0) / jnp.array([[16384.0], [4096.0]], f32) + EPSILON)[:, :, None]
    f = (((z // 4) ^ xl) * 4 + (z + y) % 4) * 2 + xh
    t_g = lax.dynamic_slice_in_dim(t_gain, f * 1024, 1024, 0).astype(f32)
    s_g = lax.dynamic_slice_in_dim(s_gain, f * 256, 256, 0).astype(f32)
    block = jnp.concatenate(
        [
            (moved[:, :1024].astype(f32) * scale[0] * t_g).astype(bf16),
            (moved[:, 1024:].astype(f32) * scale[1] * s_g).astype(bf16),
        ],
        axis=1,
    )
    block = in_order(lax.ppermute(block, ALL, TO_COLUMN), lax.ppermute(block, ALL, TO_NEXT), xh).reshape(96, 1280)

    a1, b1 = ring(block, block)
    a2, b2 = ring(a1, b1)
    a3, b3 = ring(a2, b2)
    blocks = [block, a1, a2, a3, ring_end(a3, b3), b3, b2, b1]
    tn = in_z_order([one[:, :1024] for one in blocks], z).reshape(768, 1024)
    sn = in_z_order([one[:, 1024:] for one in blocks], z).reshape(768, 256)
    tn_other, sn_other = swap_core(tn), swap_core(sn)

    def s_rows(q):
        own, other = (rows.reshape(2, 4, 96, 256)[:, q].reshape(192, 256) for rows in (sn, sn_other))
        return dot(own, s_own) + dot(other, s_other)

    s_send = [shrink(s_rows(4 - k)) for k in (1, 3)]
    s_got = [from_y(part, k) for part, k in zip(s_send, (1, 3))]
    tn, s_send = hold(tn, s_send)
    t_send = shrink(dot(tn[384:], t_own) + dot(tn_other[384:], t_other))
    t_got = from_x(t_send)
    sn, t_send = hold(sn, t_send)
    s_send = shrink(s_rows(2))
    s_got.append(from_y(s_send, 2))
    tn, sn, s_send = hold(tn, sn, s_send)
    t_keep = dot(tn[:384], t_own) + dot(tn_other[:384], t_other)
    s_keep = s_rows(0)
    t_keep, s_keep, s_got = hold(t_keep, s_keep, s_got)
    s_keep = (s_keep + sum(grow(part) for part in s_got)).reshape(2, 96, 2048)
    s_got = from_x(shrink(s_keep[1]))
    t_keep = (t_keep + grow(t_got)).reshape(4, 96, 2048)
    t_got = [from_y(shrink(t_keep[4 - k]), k) for k in (1, 3, 2)]
    s = s_keep[0] + grow(s_got)
    t = t_keep[0] + sum(grow(part) for part in t_got)

    wide_labels = labels.astype(f32)
    wanted = in_order(wide_labels, swap_core(wide_labels), c).reshape(96).astype(jnp.int32)
    ids = v * 4096 + c * 2048 + jnp.arange(2048, dtype=jnp.int32)
    hit = ids[None, :] == wanted[:, None]
    loss, grad, inner = loss_and_grad(t, s, hit, all_stats(softmax_sums(t, s, hit)))
    loss = pick(loss.reshape(2, 48), c)

    left, right = grad[:, :1024], grad[:, 1024:]
    left_got, right_got = from_x(left), from_x(right)
    far = jnp.concatenate([from_y(right, k) for k in (1, 2, 3)])
    pair = jnp.concatenate([left, left_got])
    pairs = [pair] + [from_y(pair, k) for k in (1, 2, 3)]
    right = jnp.concatenate([right, far, right_got, from_x(far)])
    inner = inner + swap_core(inner)

    over_columns = (((1,), (1,)), ((), ()))
    over_tokens = (((0,), (0,)), ((), ()))

    def inward(side, w):
        return lax.dot_general(side, w, over_columns, preferred_element_type=f32)

    def outer(rows, side):
        return lax.dot_general(rows, side, over_tokens, preferred_element_type=f32).astype(bf16)

    student = jnp.concatenate([sn, sn_other], axis=1)
    give, keep = inward(right, s_other[:, 1024:]), inward(right, s_own[:, 1024:])
    weight_right = outer(student, right)
    pairs, give, keep, inner, weight_right = hold(pairs, give, keep, inner, weight_right)
    left = jnp.concatenate([one[:96] for one in pairs] + [one[96:] for one in pairs])
    give = swap_core((give + inward(left, s_other[:, :1024])).astype(bf16))
    keep = keep + inward(left, s_own[:, :1024])
    normed_grad = (keep + give.astype(f32)).astype(bf16)
    inner = jnp.pad(inner, (0, 160)).astype(bf16)
    beside = jnp.broadcast_to(jnp.pad(inner[None], ((0, 7), (0, 0)))[None], (16, 8, 256))
    sums = jnp.concatenate([normed_grad.reshape(16, 48, 256), beside], axis=1)
    sums = lax.all_to_all(sums, VOC, split_axis=0, concat_axis=0, tiled=True)
    weight = jnp.concatenate([outer(student, left), weight_right], axis=1)
    weight_own, weight_got = weight[:256], swap_core(weight[256:])
    weight_grad = jnp.concatenate(
        [jnp.where(c == 0, weight_own, weight_got), jnp.where(c == 0, weight_got, weight_own)], axis=1
    )
    sums, weight_grad = hold(sums, weight_grad)
    sums = jnp.sum(sums.astype(f32), axis=0)
    normed_grad = lax.ppermute(lax.ppermute(sums[:48], ALL, back(TO_COLUMN)), ALL, back(TO_PLANE))
    inner = pick(sums[48, :96].reshape(2, 48), c)[:, None] / (4096.0 * scale[1])
    s_g = lax.dynamic_slice_in_dim(s_gain, v * 256, 256, 0).astype(f32)
    hidden_grad = scale[1] * (normed_grad * s_g) - s_wide * scale[1] ** 3 * inner
    return loss, hidden_grad, weight_grad


def solution(mesh):
    fine = Mesh(mesh.devices.reshape(2, 4, 2, 8, 2), ALL)
    both, rows = P(DP, VOC), P(DP)
    return jax.shard_map(
        per_device,
        mesh=fine,
        in_specs=(both, P(), both, both, P(), both, rows),
        out_specs=(rows, both, both),
        check_vma=False,
    )
```
